128 devices in a mesh: wide: 16 (over x_lo, y, core), narrow: 8 (over x_hi, z).
Axes of the slice: x: 4 (x_hi: 2, x_lo: 2; x = x_hi * 2 + x_lo), y: 4, z: 4, core: 2. Of those that a mesh axis runs over, the one named last changes fastest.
Arguments:
- coupling: bfloat16 [32768, 32768], P('wide', 'narrow'), may hold values from -0.046875 to 0.046875
- hashes: int32 [32768, 128], P(('wide', 'narrow')), may hold values from 0 to 65535
- momentum: float32 [32768, 128], P(('wide', 'narrow')), may hold values from -4 to 4
- linear: float32 [32768], P(('wide', 'narrow')), may hold values from -4 to 4
Outputs:
- positions: float32 [32768, 128], P(('wide', 'narrow'))
- velocity: float32 [32768, 128], P(('wide', 'narrow'))
The draws below stay inside these ranges and needn't reach their ends.
All inputs are finite; a program needn't handle non-finite values.
Results may differ from the reference program's by a relative error of at most 0.0037.
Values may be sent and summed in bfloat16 or wider, within the bound.
No kernel may reach another device: no remote copies, remote signals or barrier semaphores. Data moves between devices by JAX's collectives and lax.ppermute only.
A program may use at most 128 MiB of HBM per device.

```python
import jax
import jax.numpy as jnp
from jax import lax

N = 32768
REPLICAS = 128
STEPS = 4


def touch_ends(array, own_key, least, largest):
    spot = [jax.random.randint(jax.random.fold_in(own_key, axis), (), 0, length) for axis, length in enumerate(array.shape)]
    longest = array.shape.index(max(array.shape))
    neighbour = spot[:longest] + [(spot[longest] + 1) % array.shape[longest]] + spot[longest + 1:]
    return array.at[tuple(spot)].set(least).at[tuple(neighbour)].set(largest)


def raised(array, key, source, target, shards_of, factor):
    def block_of(dim):
        return (jnp.arange(array.shape[dim]) // (array.shape[dim] // shards_of)).reshape((-1,) + (1,) * (array.ndim - 1 - dim))

    one_side = jax.random.permutation(key, shards_of)[block_of(target)]
    other_side = (block_of(target) + shards_of // 2) % shards_of
    return jnp.where((block_of(source) == one_side) | (block_of(source) == other_side), factor * array, array)


def level_of(rng, dims, split, low, top_value):
    factor_of, own = 1.0, jax.random.fold_in(rng, 6)
    for axis_at, parts in split:
        heights = jnp.exp(jax.random.uniform(jax.random.fold_in(own, axis_at), (parts,), jnp.float32, low / len(split), top_value / len(split)))
        factor_of = factor_of * jnp.repeat(heights, dims[axis_at] // parts).reshape([-1 if axis == axis_at else 1 for axis in range(len(dims))])
    return factor_of


def bell_draw(key, extent, spread, bound, split=(), dtype=jnp.bfloat16):
    entries = jax.random.normal(key, extent, jnp.float32) * spread
    if len(split) > 0:
        entries = level_of(key, extent, split, -0.22, 0.18) * entries
    return jnp.clip(entries, min=-bound, max=bound).astype(dtype)


def gaussian_with(stream_key, shape, scale, limit, split, heavy, held_as=jnp.bfloat16):
    drawn = scale * jax.random.normal(stream_key, shape, jnp.float32)
    if split:
        drawn = drawn * level_of(stream_key, shape, split, -0.22, 0.18)
    return jnp.clip(raised(drawn, jax.random.fold_in(stream_key, 3), *heavy), -limit, limit).astype(held_as)


def setup_inputs(seed: int = 0) -> dict:
    streams_of = jax.random.split(jax.random.key(seed), 5)
    return {
        "coupling": gaussian_with(streams_of[0], (N, N), N ** -0.5, 0.046875, ((0, 16), (1, 8)), (1, 0, 16, 2.0)),
        "hashes": touch_ends(jax.random.randint(streams_of[1], (N, REPLICAS), 0, 65536), jax.random.fold_in(streams_of[1], 1), 0, 65535).astype(jnp.int32),
        "momentum": bell_draw(streams_of[2], (N, REPLICAS), 0.5, 4.0, ((0, 128),), jnp.float32),
        "linear": bell_draw(streams_of[3], (N,), 0.5, 4.0, ((0, 128),), jnp.float32),
    }


time_step = 1.25
coupling_scale = 0.5


def reference(coupling, hashes, momentum, linear):
    positions = (hashes.astype(jnp.float32) - 32768.0) / 65536.0
    velocity = momentum.astype(jnp.float32)
    tile_rows = min(N, 2048)
    row_tiles = coupling.reshape(N // tile_rows, tile_rows, N)
    linear_term = linear[:, None]
    for step_index in range(STEPS):
        lowered = positions.astype(jnp.bfloat16)

        def apply_tile(row_tile):
            return jnp.dot(row_tile, lowered, preferred_element_type=jnp.float32)

        local_field = lax.map(apply_tile, row_tiles).reshape(N, REPLICAS)
        pump_level = (step_index + 1.0) / (STEPS + 1.0)
        velocity = velocity + time_step * (-(1.0 - pump_level) * positions + coupling_scale * (local_field + linear_term))
        moved = positions + time_step * velocity
        clamped = jnp.clip(moved, -1.0, 1.0)
        velocity = velocity - (moved - clamped) / time_step
        positions = clamped
    return positions, velocity
```

```python
import functools

import jax
import jax.numpy as jnp
from jax import lax
from jax.experimental import pallas as pl
from jax.experimental.pallas import tpu as pltpu
from jax.sharding import PartitionSpec as P

STEPS = 4
AXES = ("wide", "narrow")

time_step = 1.25
coupling_scale = 0.5


def shifted(block, shift):
    return (block // 4 ^ shift // 4) * 4 + (block % 4 + shift % 4) % 4


def permuted(array, place, wide, narrow):
    pairs = []
    for w in range(wide):
        for n in range(narrow):
            to_w, to_n = place(w, n)
            pairs.append((w * narrow + n, to_w * narrow + to_n))
    return lax.ppermute(array, AXES, pairs)


def other_core(w, n):
    return w ^ 1, n


def to_column(turn):
    def place(w, n):
        core = w % 2
        return shifted(n, turn + 4 * core) * 2 + core, w // 2

    return place


def multiply(columns_ref, coupling_ref, *refs, add):
    *pieces, out_ref = refs
    rows = coupling_ref.shape[0]
    tile = 512

    @pl.loop(0, rows // tile)
    def _(index):
        span = pl.ds(pl.multiple_of(index * tile, tile), tile)
        if add:
            total = pieces[-1][span, :]
        else:
            total = jnp.zeros((tile, 128), jnp.float32)
        for turn in range(4):
            for half in range(2):
                first = pl.multiple_of(columns_ref[turn * 2 + half], 128)
                total += jnp.dot(
                    coupling_ref[span, pl.ds(first, 256)],
                    pieces[turn][half * 256 : half * 256 + 256, :],
                    preferred_element_type=jnp.float32,
                )
        out_ref[span, :] = total.astype(out_ref.dtype)


def product(columns, coupling, pieces, total=None):
    operands = [coupling, *pieces] + ([] if total is None else [total])
    return pl.pallas_call(
        functools.partial(multiply, add=total is not None),
        out_shape=jax.ShapeDtypeStruct((coupling.shape[0], 128), jnp.float32),
        in_specs=[pl.BlockSpec(memory_space=pltpu.SMEM)] + [pl.BlockSpec(memory_space=pltpu.VMEM)] * len(operands),
        out_specs=pl.BlockSpec(memory_space=pltpu.VMEM),
        compiler_params=pltpu.CompilerParams(vmem_limit_bytes=8 << 20),
        cost_estimate=pl.CostEstimate(flops=2 * 2048 * 2048 * 128, bytes_accessed=10 << 20, transcendentals=0),
    )(columns, *[pltpu.with_memory_space_constraint(o, pltpu.VMEM) for o in operands])


def on_device(wide, narrow, coupling, hashes, momentum, linear):
    own_w, own_n = lax.axis_index("wide"), lax.axis_index("narrow")
    block, core = own_w // 2, own_w % 2

    def columns_of(from_core):
        columns = []
        for turn in range(4):
            piece = (block // 4 ^ from_core) * 4 + (block % 4 + 4 - turn) % 4
            for half in (from_core, 1 - from_core):
                columns.append(half * 2048 + piece * 256)
        return jnp.stack(columns).astype(jnp.int32)

    own_columns, other_columns = columns_of(core), columns_of(1 - core)
    positions = (hashes.astype(jnp.float32) - 32768.0) / 65536.0
    velocity = momentum
    linear_term = linear[:, None]
    for step_index in range(STEPS):
        lowered = positions.astype(jnp.bfloat16)
        chip = jnp.concatenate([lowered, permuted(lowered, other_core, wide, narrow)])
        own = [permuted(chip, to_column(turn), wide, narrow) for turn in range(4)]
        other = [permuted(piece, other_core, wide, narrow) for piece in own]
        total = product(own_columns, coupling, own)
        partial = product(other_columns, coupling, other, total)
        sent = (partial * 256.0).astype(jnp.float16)
        parts = lax.all_to_all(sent.reshape(narrow, -1, 128), "narrow", 0, 0)
        local_field = jnp.sum(parts.astype(jnp.float32), axis=0) / 256.0
        pump_level = (step_index + 1.0) / (STEPS + 1.0)
        velocity = velocity + time_step * (
            -(1.0 - pump_level) * positions + coupling_scale * (local_field + linear_term)
        )
        moved = positions + time_step * velocity
        clamped = jnp.clip(moved, -1.0, 1.0)
        velocity = velocity - (moved - clamped) / time_step
        positions = clamped
    return (positions, velocity)


def solution(mesh):
    return jax.shard_map(
        functools.partial(on_device, mesh.shape["wide"], mesh.shape["narrow"]),
        mesh=mesh,
        in_specs=(
            P("wide", "narrow"),
            P(("wide", "narrow"), None),
            P(("wide", "narrow"), None),
            P(("wide", "narrow")),
        ),
        out_specs=(P(("wide", "narrow"), None), P(("wide", "narrow"), None)),
        check_vma=False,
    )
```

```python
import functools

import jax
import jax.numpy as jnp
from jax import lax
from jax.experimental import pallas as pl
from jax.experimental.pallas import tpu as pltpu
from jax.sharding import PartitionSpec as P

STEPS = 4
AXES = ("wide", "narrow")
REPLICAS = 128
PIECE = 256
SCALE = 256.0

time_step = 1.25
coupling_scale = 0.5


def shifted(block, shift):
    return (block // 4 ^ shift // 4) * 4 + (block % 4 + shift % 4) % 4


def permuted(array, place):
    pairs = []
    for w in range(16):
        for n in range(8):
            to_w, to_n = place(w, n)
            pairs.append((w * 8 + n, to_w * 8 + to_n))
    return lax.ppermute(array, AXES, pairs)


def other_core(w, n):
    return w ^ 1, n


def to_users(turn):
    def place(w, n):
        core = w % 2
        return shifted(n, turn + 4 * core) * 2 + core, w // 2

    return place


def multiply(wide_ref, coupling_ref, *refs, terms, add, stream):
    refs = list(refs)
    if stream:
        arrived, held_ref = refs.pop(), refs.pop()
    out_ref = refs.pop()
    total_ref = refs.pop() if add else None
    rows = out_ref.shape[0]
    tile = 512
    chip, core = wide_ref[0] // 2, wide_ref[0] % 2
    spans = []
    for turn, crossed in terms:
        sender = 1 - core if crossed else core
        piece = (chip // 4 ^ sender) * 4 + (chip % 4 + 4 - turn) % 4
        for half in (sender, 1 - sender):
            spans.append(pl.ds(pl.multiple_of(half * 2048 + piece * PIECE, PIECE), PIECE))
    copies = []
    if stream:
        for index, columns in enumerate(spans):
            copies.append(
                pltpu.make_async_copy(coupling_ref.at[:, columns], held_ref.at[index], arrived.at[index])
            )
            copies[-1].start()
    for index, piece_ref in enumerate(refs):
        for copy in copies[2 * index : 2 * index + 2]:
            copy.wait()
        for first in range(0, rows, tile):
            span = pl.ds(first, tile)
            blocks = []
            for k in (2 * index, 2 * index + 1):
                blocks.append(held_ref[k, span, :] if stream else coupling_ref[span, spans[k]])
            term = jnp.dot(blocks[0], piece_ref[:PIECE, :], preferred_element_type=jnp.float32)
            term += jnp.dot(blocks[1], piece_ref[PIECE:, :], preferred_element_type=jnp.float32)
            if index > 0:
                term += out_ref[span, :]
            elif add:
                term += total_ref[span, :]
            out_ref[span, :] = term


def product(wide, coupling, terms, pieces, total=None, stream=False):
    operands = [*pieces] + ([] if total is None else [total])
    rows = coupling.shape[0]
    depth = 2 * PIECE * len(pieces)
    space = pltpu.HBM if stream else pltpu.VMEM
    scratch = []
    if stream:
        scratch = [
            pltpu.VMEM((depth // PIECE, rows, PIECE), coupling.dtype),
            pltpu.SemaphoreType.DMA((depth // PIECE,)),
        ]
    return pl.pallas_call(
        functools.partial(multiply, terms=terms, add=total is not None, stream=stream),
        out_shape=jax.ShapeDtypeStruct((rows, REPLICAS), jnp.float32),
        in_specs=[pl.BlockSpec(memory_space=pltpu.SMEM), pl.BlockSpec(memory_space=space)]
        + [pl.BlockSpec(memory_space=pltpu.VMEM)] * len(operands),
        out_specs=pl.BlockSpec(memory_space=pltpu.VMEM),
        scratch_shapes=scratch,
        compiler_params=pltpu.CompilerParams(vmem_limit_bytes=(16 if stream else 8) << 20),
        cost_estimate=pl.CostEstimate(
            flops=2 * rows * depth * REPLICAS, bytes_accessed=rows * depth * 2, transcendentals=0
        ),
    )(wide, pltpu.with_memory_space_constraint(coupling, space), *operands)


def on_device(coupling, hashes, momentum, linear):
    wide = lax.axis_index("wide").astype(jnp.int32).reshape(1)
    positions = (hashes.astype(jnp.float32) - 32768.0) / 65536.0
    lowered = positions.astype(jnp.bfloat16)
    velocity = momentum
    linear_term = linear[:, None]
    for step_index in range(STEPS):
        chip = jnp.concatenate([lowered, permuted(lowered, other_core)])
        turns = (1, 3, 2, 0)
        own = [permuted(chip, to_users(turn)) for turn in turns]
        stream = step_index == 0
        other = [permuted(piece, other_core) for piece in own[:3]]
        total = product(wide, coupling, [(turn, False) for turn in turns[:3]], own[:3], None, stream)
        last, total = lax.optimization_barrier((own[3], total))
        other.append(permuted(last, other_core))
        terms = [(turns[3], False)] + [(turn, True) for turn in turns[:3]]
        total = product(wide, coupling, terms, [last, *other[:3]], total, stream)
        total = product(wide, coupling, [(turns[3], True)], other[3:], total, stream)
        sent = (total * SCALE).astype(jnp.float16)
        parts = lax.all_to_all(sent.reshape(8, PIECE, REPLICAS), "narrow", 0, 0)
        local_field = jnp.sum(parts.astype(jnp.float32), axis=0) / SCALE
        pump_level = (step_index + 1.0) / (STEPS + 1.0)
        velocity = velocity + time_step * (
            -(1.0 - pump_level) * positions + coupling_scale * (local_field + linear_term)
        )
        moved = positions + time_step * velocity
        clamped = jnp.clip(moved, -1.0, 1.0)
        velocity = velocity - (moved - clamped) / time_step
        positions = clamped
        lowered = positions.astype(jnp.bfloat16)
    return (positions, velocity)


def solution(mesh):
    return jax.shard_map(
        on_device,
        mesh=mesh,
        in_specs=(
            P("wide", "narrow"),
            P(("wide", "narrow"), None),
            P(("wide", "narrow"), None),
            P(("wide", "narrow")),
        ),
        out_specs=(P(("wide", "narrow"), None), P(("wide", "narrow"), None)),
        check_vma=False,
    )
```

```python
import functools

import jax
import jax.numpy as jnp
from jax import lax
from jax.experimental import pallas as pl
from jax.experimental.pallas import tpu as pltpu
from jax.sharding import PartitionSpec as P

STEPS = 4
AXES = ("wide", "narrow")
REPLICAS = 128
PIECE = 256
SCALE = 64.0

time_step = 1.25
coupling_scale = 0.5


def shifted(block, shift):
    return (block // 4 ^ shift // 4) * 4 + (block % 4 + shift % 4) % 4


def permuted(array, place):
    pairs = []
    for w in range(16):
        for n in range(8):
            to_w, to_n = place(w, n)
            pairs.append((w * 8 + n, to_w * 8 + to_n))
    return lax.ppermute(array, AXES, pairs)


def other_core(w, n):
    return w ^ 1, n


def to_users(turns):
    def place(w, n):
        core = w % 2
        return shifted(n, turns[core] + 4 * core) * 2 + core, w // 2

    return place


def to_owner(turn):
    def place(w, n):
        core = w % 2
        return w, n ^ turn ^ 4 * core

    return place


ALL, KEPT, GIVEN = range(3)


def multiply(device_ref, coupling_ref, *refs, terms, rows_of, add, stream):
    refs = list(refs)
    if stream:
        arrived, held_ref = refs.pop(), refs.pop()
    out_ref = refs.pop()
    total_ref = refs.pop() if add else None
    rows = out_ref.shape[0]
    tile = 512
    wide, narrow = device_ref[0] // 8, device_ref[0] % 8
    chip, core = wide // 2, wide % 2
    base = 0
    if rows_of != ALL:
        adder = core if rows_of == KEPT else 1 - core
        base = pl.multiple_of((narrow // 4 ^ adder) * 1024, 1024)
    spans = []
    for turns, crossed in terms:
        sender = 1 - core if crossed else core
        turn = turns[0] + (turns[1] - turns[0]) * sender
        piece = (chip // 4 ^ sender) * 4 + (chip % 4 + 4 - turn) % 4
        for half in (sender, 1 - sender):
            spans.append(pl.ds(pl.multiple_of(half * 2048 + piece * PIECE, PIECE), PIECE))
    copies = []
    if stream:
        for index, columns in enumerate(spans):
            copies.append(
                pltpu.make_async_copy(
                    coupling_ref.at[pl.ds(base, rows), columns], held_ref.at[index], arrived.at[index]
                )
            )
            copies[-1].start()
    for index, piece_ref in enumerate(refs):
        for copy in copies[2 * index : 2 * index + 2]:
            copy.wait()
        for first in range(0, rows, tile):
            blocks = []
            for k in (2 * index, 2 * index + 1):
                if stream:
                    blocks.append(held_ref[k, pl.ds(first, tile), :])
                else:
                    blocks.append(coupling_ref[pl.ds(base + first, tile), spans[k]])
            term = jnp.dot(blocks[0], piece_ref[:PIECE, :], preferred_element_type=jnp.float32)
            term += jnp.dot(blocks[1], piece_ref[PIECE:, :], preferred_element_type=jnp.float32)
            for begin in range(0, tile, PIECE):
                to = first + begin
                if rows_of != ALL:
                    to = pl.multiple_of((narrow % 4 ^ to // PIECE) * PIECE, PIECE)
                to = pl.ds(to, PIECE)
                here = term[begin : begin + PIECE, :]
                if index > 0:
                    here += out_ref[to, :]
                elif add and total_ref.shape[0] == rows:
                    here += total_ref[to, :]
                elif add:
                    here += total_ref[pl.ds(base + first + begin, PIECE), :]
                out_ref[to, :] = here


def product(device, coupling, terms, pieces, total=None, rows_of=ALL, stream=False):
    operands = [*pieces] + ([] if total is None else [total])
    rows = coupling.shape[0] if rows_of == ALL else 1024
    depth = 2 * PIECE * len(pieces)
    space = pltpu.HBM if stream else pltpu.VMEM
    scratch = []
    if stream:
        scratch = [
            pltpu.VMEM((depth // PIECE, rows, PIECE), coupling.dtype),
            pltpu.SemaphoreType.DMA((depth // PIECE,)),
        ]
    return pl.pallas_call(
        functools.partial(multiply, terms=terms, rows_of=rows_of, add=total is not None, stream=stream),
        out_shape=jax.ShapeDtypeStruct((rows, REPLICAS), jnp.float32),
        in_specs=[pl.BlockSpec(memory_space=pltpu.SMEM), pl.BlockSpec(memory_space=space)]
        + [pl.BlockSpec(memory_space=pltpu.VMEM)] * len(operands),
        out_specs=pl.BlockSpec(memory_space=pltpu.VMEM),
        scratch_shapes=scratch,
        compiler_params=pltpu.CompilerParams(vmem_limit_bytes=(16 if stream else 8) << 20),
        cost_estimate=pl.CostEstimate(
            flops=2 * rows * depth * REPLICAS, bytes_accessed=rows * depth * 2, transcendentals=0
        ),
    )(device, pltpu.with_memory_space_constraint(coupling, space), *operands)


def on_device(coupling, hashes, momentum, linear):
    device = (lax.axis_index("wide") * 8 + lax.axis_index("narrow")).astype(jnp.int32).reshape(1)
    positions = (hashes.astype(jnp.float32) - 32768.0) / 65536.0
    velocity, linear_term = momentum, linear[:, None]
    lowered = positions.astype(jnp.bfloat16)
    lowered = jnp.concatenate([lowered, permuted(lowered, other_core)])
    turns = ((0, 1), (1, 3), (3, 2), (2, 0))
    for step_index in range(STEPS):
        own = [permuted(lowered, to_users(turn)) for turn in turns]
        stream = step_index == 0
        if step_index == STEPS - 1:
            positions, velocity, linear_term = positions[:PIECE], velocity[:PIECE], linear_term[:PIECE]
        others = [permuted(piece, other_core) for piece in own[:3]]
        total = product(device, coupling, [(turn, False) for turn in turns[:3]], own[:3], None, ALL, stream)
        last, total = lax.optimization_barrier((own[3], total))
        late = permuted(last, other_core)
        terms = [(turns[3], False)] + [(turn, True) for turn in turns[:3]]
        end = [(turns[3], True)]
        if step_index == 0:
            total = product(device, coupling, terms, [last, *others], total, ALL, stream)
            total = product(device, coupling, end, [late], total, ALL, stream)
            sent = (total * SCALE).astype(jnp.float16)
            parts = lax.all_to_all(sent.reshape(8, PIECE, REPLICAS), "narrow", 0, 0)
            field = jnp.sum(parts.astype(jnp.float32), axis=0)
        else:
            given = product(device, coupling, terms, [last, *others], total, GIVEN)
            given = product(device, coupling, end, [late], given, GIVEN)
            given = permuted((given * SCALE).astype(jnp.float16), other_core)
            kept = product(device, coupling, terms + end, [last, *others, late], total, KEPT)
            kept = (kept * SCALE).astype(jnp.float16)
            sums = []
            for turn in (2, 1, 3, 0):
                rows = slice(turn * PIECE, turn * PIECE + PIECE)
                sums.append(permuted(jnp.concatenate([kept[rows], given[rows]]), to_owner(turn)))
            half_sum = lax.optimization_barrier(sum(part.astype(jnp.float32) for part in sums).astype(jnp.float16))
            if step_index == STEPS - 1:
                field = half_sum[:PIECE].astype(jnp.float32)
                field += permuted(half_sum[PIECE:], other_core).astype(jnp.float32)
            else:
                theirs = permuted(half_sum, other_core)
                theirs = jnp.concatenate([theirs[PIECE:], theirs[:PIECE]])
                field = half_sum.astype(jnp.float32) + theirs.astype(jnp.float32)
        local_field = field / SCALE
        pump_level = (step_index + 1.0) / (STEPS + 1.0)
        velocity = velocity + time_step * (
            -(1.0 - pump_level) * positions + coupling_scale * (local_field + linear_term)
        )
        moved = positions + time_step * velocity
        clamped = jnp.clip(moved, -1.0, 1.0)
        velocity = velocity - (moved - clamped) / time_step
        positions = clamped
        lowered = positions.astype(jnp.bfloat16)
        if step_index == 0:
            lowered = jnp.concatenate([lowered, permuted(lowered, other_core)])
            state = jnp.concatenate([positions, velocity, jnp.pad(linear.reshape(2, 128), ((0, 6), (0, 0)))])
            both = [state, permuted(state, other_core)]
            positions, velocity = (jnp.concatenate([s[k : k + PIECE] for s in both]) for k in (0, PIECE))
            linear_term = jnp.concatenate([s[2 * PIECE : 2 * PIECE + 2].reshape(PIECE) for s in both])[:, None]
    return (positions, velocity)


def solution(mesh):
    return jax.shard_map(
        on_device,
        mesh=mesh,
        in_specs=(
            P("wide", "narrow"),
            P(("wide", "narrow"), None),
            P(("wide", "narrow"), None),
            P(("wide", "narrow")),
        ),
        out_specs=(P(("wide", "narrow"), None), P(("wide", "narrow"), None)),
        check_vma=False,
    )
```

```python
import functools

import jax
import jax.numpy as jnp
from jax import lax
from jax.experimental import pallas as pl
from jax.experimental.pallas import tpu as pltpu
from jax.sharding import PartitionSpec as P

STEPS = 4
AXES = ("wide", "narrow")
REPLICAS = 128
PIECE = 256
SCALE = 64.0

time_step = 1.25
coupling_scale = 0.5


def shifted(block, shift):
    return (block // 4 ^ shift // 4) * 4 + (block % 4 + shift % 4) % 4


def permuted(array, place):
    pairs = []
    for w in range(16):
        for n in range(8):
            to_w, to_n = place(w, n)
            pairs.append((w * 8 + n, to_w * 8 + to_n))
    return lax.ppermute(array, AXES, pairs)


def other_core(w, n):
    return w ^ 1, n


def to_users(turns):
    def place(w, n):
        core = w % 2
        return shifted(n, turns[core] + 4 * core) * 2 + core, w // 2

    return place


def to_owner(turn):
    def place(w, n):
        core = w % 2
        return w, n ^ turn ^ 4 * core

    return place


ALL, KEPT, GIVEN = range(3)


def multiply(device_ref, coupling_ref, *refs, terms, rows_of, add, stream):
    refs = list(refs)
    if stream:
        arrived, held_ref = refs.pop(), refs.pop()
    out_ref = refs.pop()
    total_ref = refs.pop() if add else None
    rows = out_ref.shape[0]
    tile = 512
    wide, narrow = device_ref[0] // 8, device_ref[0] % 8
    chip, core = wide // 2, wide % 2
    base = 0
    if rows_of != ALL:
        adder = core if rows_of == KEPT else 1 - core
        base = pl.multiple_of((narrow // 4 ^ adder) * 1024, 1024)
    spans = []
    for turns, crossed in terms:
        sender = 1 - core if crossed else core
        turn = turns[0] + (turns[1] - turns[0]) * sender
        piece = (chip // 4 ^ sender) * 4 + (chip % 4 + 4 - turn) % 4
        for half in (sender, 1 - sender):
            spans.append(pl.ds(pl.multiple_of(half * 2048 + piece * PIECE, PIECE), PIECE))
    copies = []
    if stream:
        for index, columns in enumerate(spans):
            copies.append(
                pltpu.make_async_copy(
                    coupling_ref.at[pl.ds(base, rows), columns], held_ref.at[index], arrived.at[index]
                )
            )
            copies[-1].start()
    for index, piece_ref in enumerate(refs):
        for copy in copies[2 * index : 2 * index + 2]:
            copy.wait()
        for first in range(0, rows, tile):
            blocks = []
            for k in (2 * index, 2 * index + 1):
                if stream:
                    blocks.append(held_ref[k, pl.ds(first, tile), :])
                else:
                    blocks.append(coupling_ref[pl.ds(base + first, tile), spans[k]])
            term = jnp.dot(blocks[0], piece_ref[:PIECE, :], preferred_element_type=jnp.float32)
            term += jnp.dot(blocks[1], piece_ref[PIECE:, :], preferred_element_type=jnp.float32)
            for begin in range(0, tile, PIECE):
                to = first + begin
                if rows_of != ALL:
                    to = pl.multiple_of((narrow % 4 ^ to // PIECE) * PIECE, PIECE)
                to = pl.ds(to, PIECE)
                here = term[begin : begin + PIECE, :]
                if index > 0:
                    here += out_ref[to, :]
                elif add and total_ref.shape[0] == rows:
                    here += total_ref[to, :]
                elif add:
                    here += total_ref[pl.ds(base + first + begin, PIECE), :]
                out_ref[to, :] = here


def product(device, coupling, terms, pieces, total=None, rows_of=ALL, stream=False):
    operands = [*pieces] + ([] if total is None else [total])
    rows = coupling.shape[0] if rows_of == ALL else 1024
    depth = 2 * PIECE * len(pieces)
    space = pltpu.HBM if stream else pltpu.VMEM
    scratch = []
    if stream:
        scratch = [
            pltpu.VMEM((depth // PIECE, rows, PIECE), coupling.dtype),
            pltpu.SemaphoreType.DMA((depth // PIECE,)),
        ]
    return pl.pallas_call(
        functools.partial(multiply, terms=terms, rows_of=rows_of, add=total is not None, stream=stream),
        out_shape=jax.ShapeDtypeStruct((rows, REPLICAS), jnp.float32),
        in_specs=[pl.BlockSpec(memory_space=pltpu.SMEM), pl.BlockSpec(memory_space=space)]
        + [pl.BlockSpec(memory_space=pltpu.VMEM)] * len(operands),
        out_specs=pl.BlockSpec(memory_space=pltpu.VMEM),
        scratch_shapes=scratch,
        compiler_params=pltpu.CompilerParams(vmem_limit_bytes=(16 if stream else 8) << 20),
        cost_estimate=pl.CostEstimate(
            flops=2 * rows * depth * REPLICAS, bytes_accessed=rows * depth * 2, transcendentals=0
        ),
    )(device, pltpu.with_memory_space_constraint(coupling, space), *operands)


def on_device(coupling, hashes, momentum, linear):
    device = (lax.axis_index("wide") * 8 + lax.axis_index("narrow")).astype(jnp.int32).reshape(1)
    positions = (hashes.astype(jnp.float32) - 32768.0) / 65536.0
    velocity, linear_term = momentum, linear[:, None]
    lowered = positions.astype(jnp.bfloat16)
    lowered = jnp.concatenate([lowered, permuted(lowered, other_core)])
    turns = ((0, 1), (1, 3), (3, 2), (2, 0))
    for step_index in range(STEPS):
        own = [permuted(lowered, to_users(turn)) for turn in turns]
        stream = step_index == 0
        if step_index == STEPS - 1:
            positions, velocity, linear_term = positions[:PIECE], velocity[:PIECE], linear_term[:PIECE]
        others = [permuted(piece, other_core) for piece in own[:3]]
        total = product(device, coupling, [(turn, False) for turn in turns[:3]], own[:3], None, ALL, stream)
        last, total = lax.optimization_barrier((own[3], total))
        late = permuted(last, other_core)
        terms = [(turns[3], False)] + [(turn, True) for turn in turns[:3]]
        end = [(turns[3], True)]
        if step_index in (0, STEPS - 1):
            total = product(device, coupling, terms, [last, *others], total, ALL, stream)
            total = product(device, coupling, end, [late], total, ALL, stream)
            sent = (total * SCALE).astype(jnp.float16)
            parts = lax.all_to_all(sent.reshape(8, PIECE, REPLICAS), "narrow", 0, 0)
            field = jnp.sum(parts.astype(jnp.float32), axis=0)
        else:
            given = product(device, coupling, terms, [last, *others], total, GIVEN)
            given = product(device, coupling, end, [late], given, GIVEN)
            given = permuted((given * SCALE).astype(jnp.float16), other_core)
            kept = product(device, coupling, terms + end, [last, *others, late], total, KEPT)
            kept = (kept * SCALE).astype(jnp.float16)
            sums = []
            for turn in (2, 1, 3, 0):
                rows = slice(turn * PIECE, turn * PIECE + PIECE)
                sums.append(permuted(jnp.concatenate([kept[rows], given[rows]]), to_owner(turn)))
            half_sum = lax.optimization_barrier(sum(part.astype(jnp.float32) for part in sums).astype(jnp.float16))
            theirs = permuted(half_sum, other_core)
            theirs = jnp.concatenate([theirs[PIECE:], theirs[:PIECE]])
            field = half_sum.astype(jnp.float32) + theirs.astype(jnp.float32)
        local_field = field / SCALE
        pump_level = (step_index + 1.0) / (STEPS + 1.0)
        velocity = velocity + time_step * (
            -(1.0 - pump_level) * positions + coupling_scale * (local_field + linear_term)
        )
        moved = positions + time_step * velocity
        clamped = jnp.clip(moved, -1.0, 1.0)
        velocity = velocity - (moved - clamped) / time_step
        positions = clamped
        lowered = positions.astype(jnp.bfloat16)
        if step_index == 0:
            lowered = jnp.concatenate([lowered, permuted(lowered, other_core)])
            state = jnp.concatenate([positions, velocity, jnp.pad(linear.reshape(2, 128), ((0, 6), (0, 0)))])
            both = [state, permuted(state, other_core)]
            positions, velocity = (jnp.concatenate([s[k : k + PIECE] for s in both]) for k in (0, PIECE))
            linear_term = jnp.concatenate([s[2 * PIECE : 2 * PIECE + 2].reshape(PIECE) for s in both])[:, None]
    return (positions, velocity)


def solution(mesh):
    return jax.shard_map(
        on_device,
        mesh=mesh,
        in_specs=(
            P("wide", "narrow"),
            P(("wide", "narrow"), None),
            P(("wide", "narrow"), None),
            P(("wide", "narrow")),
        ),
        out_specs=(P(("wide", "narrow"), None), P(("wide", "narrow"), None)),
        check_vma=False,
    )
```

```python
import functools

import jax
import jax.numpy as jnp
from jax import lax
from jax.experimental import pallas as pl
from jax.experimental.pallas import tpu as pltpu
from jax.sharding import PartitionSpec as P

STEPS = 4
AXES = ("wide", "narrow")
REPLICAS = 128
PIECE = 256
SCALE = 64.0

time_step = 1.25
coupling_scale = 0.5


def shifted(block, shift):
    return (block // 4 ^ shift // 4) * 4 + (block % 4 + shift % 4) % 4


def permuted(array, place):
    pairs = []
    for w in range(16):
        for n in range(8):
            to_w, to_n = place(w, n)
            pairs.append((w * 8 + n, to_w * 8 + to_n))
    return lax.ppermute(array, AXES, pairs)


def other_core(w, n):
    return w ^ 1, n


def to_users(turns):
    def place(w, n):
        core = w % 2
        return shifted(n, turns[core] + 4 * core) * 2 + core, w // 2

    return place


def to_owner(turn):
    def place(w, n):
        core = w % 2
        return w, n ^ turn ^ 4 * core

    return place


ALL, KEPT, GIVEN = range(3)


def multiply(device_ref, coupling_ref, *refs, terms, rows_of, add, stream):
    refs = list(refs)
    if stream:
        arrived, held_ref = refs.pop(), refs.pop()
    out_ref = refs.pop()
    total_ref = refs.pop() if add else None
    rows = out_ref.shape[0]
    tile = 512
    wide, narrow = device_ref[0] // 8, device_ref[0] % 8
    chip, core = wide // 2, wide % 2
    base = 0
    if rows_of != ALL:
        adder = core if rows_of == KEPT else 1 - core
        base = pl.multiple_of((narrow // 4 ^ adder) * 1024, 1024)
    spans = []
    for turns, crossed in terms:
        sender = 1 - core if crossed else core
        turn = turns[0] + (turns[1] - turns[0]) * sender
        piece = (chip // 4 ^ sender) * 4 + (chip % 4 + 4 - turn) % 4
        for half in (sender, 1 - sender):
            spans.append(pl.ds(pl.multiple_of(half * 2048 + piece * PIECE, PIECE), PIECE))
    copies = []
    if stream:
        for index, columns in enumerate(spans):
            copies.append(
                pltpu.make_async_copy(
                    coupling_ref.at[pl.ds(base, rows), columns], held_ref.at[index], arrived.at[index]
                )
            )
            copies[-1].start()
    for index, piece_ref in enumerate(refs):
        for copy in copies[2 * index : 2 * index + 2]:
            copy.wait()
        for first in range(0, rows, tile):
            blocks = []
            for k in (2 * index, 2 * index + 1):
                if stream:
                    blocks.append(held_ref[k, pl.ds(first, tile), :])
                else:
                    blocks.append(coupling_ref[pl.ds(base + first, tile), spans[k]])
            term = jnp.dot(blocks[0], piece_ref[:PIECE, :], preferred_element_type=jnp.float32)
            term += jnp.dot(blocks[1], piece_ref[PIECE:, :], preferred_element_type=jnp.float32)
            for begin in range(0, tile, PIECE):
                to = first + begin
                if rows_of != ALL:
                    to = pl.multiple_of((narrow % 4 ^ to // PIECE) * PIECE, PIECE)
                to = pl.ds(to, PIECE)
                here = term[begin : begin + PIECE, :]
                if index > 0:
                    here += out_ref[to, :]
                elif add and total_ref.shape[0] == rows:
                    here += total_ref[to, :]
                elif add:
                    here += total_ref[pl.ds(base + first + begin, PIECE), :]
                out_ref[to, :] = here


def product(device, coupling, terms, pieces, total=None, rows_of=ALL, stream=False):
    operands = [*pieces] + ([] if total is None else [total])
    rows = coupling.shape[0] if rows_of == ALL else 1024
    depth = 2 * PIECE * len(pieces)
    space = pltpu.HBM if stream else pltpu.VMEM
    scratch = []
    if stream:
        scratch = [
            pltpu.VMEM((depth // PIECE, rows, PIECE), coupling.dtype),
            pltpu.SemaphoreType.DMA((depth // PIECE,)),
        ]
    return pl.pallas_call(
        functools.partial(multiply, terms=terms, rows_of=rows_of, add=total is not None, stream=stream),
        out_shape=jax.ShapeDtypeStruct((rows, REPLICAS), jnp.float32),
        in_specs=[pl.BlockSpec(memory_space=pltpu.SMEM), pl.BlockSpec(memory_space=space)]
        + [pl.BlockSpec(memory_space=pltpu.VMEM)] * len(operands),
        out_specs=pl.BlockSpec(memory_space=pltpu.VMEM),
        scratch_shapes=scratch,
        compiler_params=pltpu.CompilerParams(vmem_limit_bytes=(16 if stream else 8) << 20),
        cost_estimate=pl.CostEstimate(
            flops=2 * rows * depth * REPLICAS, bytes_accessed=rows * depth * 2, transcendentals=0
        ),
    )(device, pltpu.with_memory_space_constraint(coupling, space), *operands)


def on_device(coupling, hashes, momentum, linear):
    device = (lax.axis_index("wide") * 8 + lax.axis_index("narrow")).astype(jnp.int32).reshape(1)
    theirs = permuted(hashes, other_core)
    positions, other_positions = ((h.astype(jnp.float32) - 32768.0) / 65536.0 for h in (hashes, theirs))
    velocity, linear_term = momentum, linear[:, None]
    lowered = jnp.concatenate([positions.astype(jnp.bfloat16), other_positions.astype(jnp.bfloat16)])
    turns = ((0, 1), (1, 3), (3, 2), (2, 0))
    for step_index in range(STEPS):
        own = [permuted(lowered, to_users(turn)) for turn in turns]
        stream = step_index == 0
        if step_index == STEPS - 1:
            positions, velocity, linear_term = positions[:PIECE], velocity[:PIECE], linear_term[:PIECE]
        others = [permuted(piece, other_core) for piece in own[:3]]
        total = product(device, coupling, [(turn, False) for turn in turns[:3]], own[:3], None, ALL, stream)
        last, total = lax.optimization_barrier((own[3], total))
        late = permuted(last, other_core)
        terms = [(turns[3], False)] + [(turn, True) for turn in turns[:3]]
        end = [(turns[3], True)]
        if step_index in (0, STEPS - 1):
            total = product(device, coupling, terms, [last, *others], total, ALL, stream)
            total = product(device, coupling, end, [late], total, ALL, stream)
            sent = (total * SCALE).astype(jnp.float16)
            parts = lax.all_to_all(sent.reshape(8, PIECE, REPLICAS), "narrow", 0, 0)
            field = jnp.sum(parts.astype(jnp.float32), axis=0)
        else:
            given = product(device, coupling, terms, [last, *others], total, GIVEN)
            given = product(device, coupling, end, [late], given, GIVEN)
            given = permuted((given * SCALE).astype(jnp.float16), other_core)
            kept = product(device, coupling, terms + end, [last, *others, late], total, KEPT)
            kept = (kept * SCALE).astype(jnp.float16)
            sums = []
            for turn in (2, 1, 3, 0):
                rows = slice(turn * PIECE, turn * PIECE + PIECE)
                sums.append(permuted(jnp.concatenate([kept[rows], given[rows]]), to_owner(turn)))
            half_sum = lax.optimization_barrier(sum(part.astype(jnp.float32) for part in sums).astype(jnp.float16))
            theirs = permuted(half_sum, other_core)
            theirs = jnp.concatenate([theirs[PIECE:], theirs[:PIECE]])
            field = half_sum.astype(jnp.float32) + theirs.astype(jnp.float32)
        local_field = field / SCALE
        pump_level = (step_index + 1.0) / (STEPS + 1.0)
        velocity = velocity + time_step * (
            -(1.0 - pump_level) * positions + coupling_scale * (local_field + linear_term)
        )
        moved = positions + time_step * velocity
        clamped = jnp.clip(moved, -1.0, 1.0)
        velocity = velocity - (moved - clamped) / time_step
        positions = clamped
        lowered = positions.astype(jnp.bfloat16)
        if step_index == 0:
            lowered = jnp.concatenate([lowered, permuted(lowered, other_core)])
            state = jnp.concatenate([positions, velocity, jnp.pad(linear.reshape(2, 128), ((0, 6), (0, 0)))])
            both = [state, permuted(state, other_core)]
            positions, velocity = (jnp.concatenate([s[k : k + PIECE] for s in both]) for k in (0, PIECE))
            linear_term = jnp.concatenate([s[2 * PIECE : 2 * PIECE + 2].reshape(PIECE) for s in both])[:, None]
    return (positions, velocity)


def solution(mesh):
    return jax.shard_map(
        on_device,
        mesh=mesh,
        in_specs=(
            P("wide", "narrow"),
            P(("wide", "narrow"), None),
            P(("wide", "narrow"), None),
            P(("wide", "narrow")),
        ),
        out_specs=(P(("wide", "narrow"), None), P(("wide", "narrow"), None)),
        check_vma=False,
    )
```
